32 devices in a mesh: seq: 8 (over z, y), tensor: 4 (over x, core).
Axes of the slice: x: 2, y: 2, z: 4, core: 2. Of those that a mesh axis runs over, the one named last changes fastest.
Arguments:
- stream: bfloat16 [32, 2304], P('seq'), may hold values from -6 to 6
- new_query: bfloat16 [32, 2304], P('seq', 'tensor'), may hold values from -13 to 13
- k_new: bfloat16 [32, 2304], P('seq', 'tensor'), may hold values from -5 to 5
- v_new: bfloat16 [32, 2304], P('seq', 'tensor'), may hold values from -5 to 5
- k_cache: bfloat16 [32, 64, 2304], P('seq', None, 'tensor'), may hold values from -4 to 4
- v_cache: bfloat16 [32, 64, 2304], P('seq', None, 'tensor'), may hold values from -5 to 5
- page_owner: int32 [32], replicated, may hold values from 0 to 31
- page_fill: int32 [32], P('seq'), may hold values from 2 to 64
- out_weight: bfloat16 [2304, 2304], P('tensor', 'seq'), may hold values from -0.125 to 0.125
- norm_gain: float32 [2304], replicated, may hold values from 0.5 to 1.5
- routes: int32 [32, 2], P('seq'), may hold values from 0 to 7, all different within a row; in each aligned block of 4 rows (0 to 3, 4 to 7, ...) at most 2 rows name the same one
- route_weight: float32 [32, 2], P('seq'), may hold values from 0.2 to 1
- w_gate: bfloat16 [8, 2304, 5760], P('seq', 'tensor'), may hold values from -0.125 to 0.125
- w_up: bfloat16 [8, 2304, 5760], P('seq', 'tensor'), may hold values from -0.125 to 0.125
- w_down: bfloat16 [8, 5760, 2304], P('seq', None, 'tensor'), may hold values from -0.078125 to 0.078125
Outputs:
- attn_out: bfloat16 [32, 2304], P('seq', 'tensor')
- moe_out: bfloat16 [32, 2304], P('seq', 'tensor')
The draws below stay inside these ranges and needn't reach their ends.
Inputs may be any that keep to these rules, and one draw needn't show every extreme that they name: `routes`: each request names 2 different experts; among the 4 requests of one index of seq (an aligned block) no expert is named more than 2 times, and in some blocks one is named exactly 2 times.
All inputs are finite; a program needn't handle non-finite values.
Results may differ from the reference program's by a relative error of at most 0.012.
Values may be sent and summed in bfloat16 or wider, within the bound.
A program may use at most 64 MiB of HBM per device.

```python
import math
import jax
import jax.numpy as jnp
import numpy as np
from jax import lax

D = 2304
HEADS = 36
HEAD_DIM = 64
EXPERTS = 8
TOP = 2
FF = 5760
PAGE_LEN = 64
REQ_DEV = 4
REQUESTS = 32
PAGES = 32
SLICES = 1
FF_SLICE = 5760
CAP = 2
N_SEQ = 8


def drawn_signs(key):
    bits = jax.random.randint(jax.random.fold_in(key, 3), (HEADS * HEAD_DIM,), 0, 2)
    return bits.astype(jnp.float32) * 2.0 - 1.0


def draw_new_query(key, part):
    signs = drawn_signs(key)
    inner = jax.random.fold_in(key, 1)
    base = jnp.clip(jax.random.normal(inner, (REQUESTS, HEADS * HEAD_DIM), jnp.float32), -4.0, 4.0)
    rows = jnp.arange(REQUESTS)
    strength = 11.0 + (rows // 4 % 3).astype(jnp.float32)
    picked = rows % 4 == 3
    out = jnp.where(picked[:, None], strength[:, None] * signs[None, :], base)
    return out.astype(jnp.bfloat16)


def draw_k_cache(key, part):
    signs = drawn_signs(key)
    inner = jax.random.fold_in(key, 2)
    shape = (PAGES, PAGE_LEN, HEADS * HEAD_DIM)
    base = jnp.clip(jax.random.normal(inner, shape, jnp.float32), -4.0, 4.0)
    slots = jnp.arange(PAGE_LEN)
    level = jnp.where(slots == 0, 4.0, 3.96875)
    picked = slots < 2
    out = jnp.where(picked[None, :, None], level[None, :, None] * signs[None, None, :], base)
    return out.astype(jnp.bfloat16)


def plant(drawn, stream_key, low, largest):
    index_at = [jax.random.randint(jax.random.fold_in(stream_key, axis), (), 0, length) for axis, length in enumerate(drawn.shape)]
    main_axis = drawn.shape.index(max(drawn.shape))
    neighbour = index_at[:main_axis] + [(index_at[main_axis] + 1) % drawn.shape[main_axis]] + index_at[main_axis + 1:]
    return drawn.at[tuple(index_at)].set(low).at[tuple(neighbour)].set(largest)


def block_levels(own_key, dims, cuts, low, largest):
    factor_of = 1.0
    for dim, shards_of in cuts:
        draws = jax.random.uniform(jax.random.fold_in(jax.random.fold_in(own_key, 6), dim), (shards_of,), jnp.float32, low / len(cuts), largest / len(cuts))
        factor_of = factor_of * jnp.repeat(jnp.exp(draws), dims[dim] // shards_of).reshape((-1,) + (1,) * (len(dims) - 1 - dim))
    return factor_of


def routed_block(stream_key, own, number, rows, count, top, bound, skew):
    order = jax.random.permutation(stream_key, count)
    crowded, common = portions_of(count, rows * top, bound, skew, True), portions_of(count, rows * top, bound, skew, False)
    places = jnp.arange(count)

    def named(lengths, rotation):
        used = int((lengths > 0).sum())
        fixed = max(1, used // 4)
        shifted = fixed + (places - fixed + rotation * (used - fixed)) % max(1, count - fixed)
        return jnp.zeros((count,), jnp.int32).at[order[jnp.where(places < fixed, places, shifted)]].set(jnp.asarray(lengths, jnp.int32))

    lengths = jnp.where(number % 4 == 0, named(crowded, number // 4), named(common, number - number // 4 - 1))
    mixed = jax.random.permutation(jax.random.fold_in(own, 3), count)
    giver, taker = mixed[0:count // 2 * 2:2], mixed[1:count // 2 * 2:2]
    room = jnp.minimum(lengths[giver] - 1, bound - lengths[taker]) // 2
    room = jnp.where((giver == order[0]) | (taker == order[0]) | (lengths[taker] == 0), 0, jnp.maximum(room, 0))
    shifted = jax.random.randint(jax.random.fold_in(own, 4), (count // 2,), 0, 1 << 20) % (room + 1)
    lengths = lengths.at[giver].add(-shifted).at[taker].add(shifted)
    members = jnp.searchsorted(jnp.cumsum(lengths), jnp.arange(rows * top), side="right").astype(jnp.int32)
    table = members.reshape(top, rows).T
    table = table[jax.random.permutation(jax.random.fold_in(own, 1), rows)]
    rotation = jax.random.randint(jax.random.fold_in(own, 2), (rows, 1), 0, top)
    return jnp.take_along_axis(table, (jnp.arange(top)[None, :] + rotation) % top, axis=1)


def portions_of(number_of, total, bound, skew, full):
    loads = [(1 << 20) // math.isqrt(rank ** skew) + 1 for rank in range(1, number_of + 1)]
    largest = bound if full else min(bound, max(-(-total // number_of), total * loads[0] // sum(loads)))
    least = 1 if total - largest >= number_of - 1 else 0
    holding, rest = [largest] + [least] * (number_of - 1), total - largest - least * (number_of - 1)
    while rest > 0:
        movable = [i for i in range(1, number_of) if holding[i] < largest] or [i for i in range(1, number_of) if holding[i] < bound]
        pool, remaining = sum([loads[i] for i in movable]), rest
        for i in movable:
            addition = min(bound - holding[i], max(1, remaining * loads[i] // pool), rest)
            holding[i] = holding[i] + addition
            rest = rest - addition
    return np.array(holding)


def normal_values(stream_key, dims, scale, most, split=(), kind=jnp.bfloat16):
    array = scale * jax.random.normal(stream_key, dims, jnp.float32)
    if split:
        array = array * block_levels(stream_key, dims, split, -0.22, 0.18)
    return jnp.clip(array, -most, most).astype(kind)


def setup_inputs(seed: int = 0) -> dict:
    splits = jax.random.split(jax.random.key(seed), 16)
    stream = normal_values(splits[0], (REQUESTS, D), 1.0, 6.0, ((0, 8),))
    new_query = draw_new_query(jax.random.fold_in(splits[15], 71), 0)
    k_new = normal_values(splits[2], (REQUESTS, HEADS * HEAD_DIM), 1.0, 5.0, ((0, 8), (1, 4)))
    v_new = normal_values(splits[3], (REQUESTS, HEADS * HEAD_DIM), 1.0, 5.0, ((0, 8), (1, 4)))
    k_cache = draw_k_cache(jax.random.fold_in(splits[15], 71), 0)
    v_cache = normal_values(splits[5], (PAGES, PAGE_LEN, HEADS * HEAD_DIM), 1.0, 5.0, ((0, 8), (2, 4)))
    page_owner = plant(jax.random.randint(splits[6], (PAGES,), 0, REQUESTS), jax.random.fold_in(splits[6], 1), 0, REQUESTS - 1).astype(jnp.int32)
    page_fill = plant(jax.random.randint(splits[7], (PAGES,), 2, PAGE_LEN + 1), jax.random.fold_in(splits[7], 1), 2, PAGE_LEN).astype(jnp.int32)
    out_weight = normal_values(splits[8], (HEADS * HEAD_DIM, D), (HEADS * HEAD_DIM) ** -0.5, 0.125, ((0, 4), (1, 8)))
    norm_gain = jnp.clip(1.0 + 0.1 * jax.random.normal(splits[9], (D,), jnp.float32), 0.5, 1.5)
    routes_keys = jax.random.split(jax.random.fold_in(splits[10], 1), REQUESTS // REQ_DEV)
    routes_turns = jax.random.permutation(jax.random.fold_in(splits[10], 3), REQUESTS // REQ_DEV)
    routes = jax.vmap(lambda own, number: routed_block(jax.random.fold_in(splits[10], 2), own, number, REQ_DEV, EXPERTS, TOP, CAP, 2))(routes_keys, routes_turns).reshape((REQUESTS, TOP))
    route_weight = jnp.clip(0.2 + 0.8 * jax.random.uniform(splits[11], (REQUESTS, TOP), jnp.float32) ** block_levels(splits[11], (REQUESTS, TOP), ((0, 8),), -0.2, 0.2), 0.2, 1.0)
    w_gate = normal_values(splits[12], (EXPERTS * SLICES, D, FF_SLICE), D ** -0.5, 0.125, ((0, 8), (1, 4)))
    w_up = normal_values(splits[13], (EXPERTS * SLICES, D, FF_SLICE), D ** -0.5, 0.125, ((0, 8), (1, 4)))
    w_down = normal_values(splits[14], (EXPERTS * SLICES, FF_SLICE, D), FF ** -0.5, 0.078125, ((0, 8), (2, 4)))
    return dict(stream=stream, new_query=new_query, k_new=k_new, v_new=v_new, k_cache=k_cache, v_cache=v_cache, page_owner=page_owner, page_fill=page_fill, out_weight=out_weight, norm_gain=norm_gain, routes=routes, route_weight=route_weight, w_gate=w_gate, w_up=w_up, w_down=w_down)


def reference(stream, new_query, k_new, v_new, k_cache, v_cache, page_owner, page_fill, out_weight, norm_gain, routes, route_weight, w_gate, w_up, w_down):
    scale = 1.0 / HEAD_DIM ** 0.5
    queries = new_query.astype(jnp.float32).reshape(REQUESTS, HEADS, HEAD_DIM)
    keys = k_cache.astype(jnp.float32).reshape(PAGES, PAGE_LEN, HEADS, HEAD_DIM)
    values = v_cache.astype(jnp.float32).reshape(PAGES, PAGE_LEN, HEADS, HEAD_DIM)
    page_queries = jnp.take(queries, page_owner, axis=0)
    scores = jnp.einsum('phd,pjhd->phj', page_queries, keys) * scale
    valid = jnp.arange(PAGE_LEN, dtype=jnp.int32)[None, :] < page_fill[:, None]
    scores = jnp.where(valid[:, None, :], scores, jnp.float32(-1e+30))
    own = lax.optimization_barrier(jnp.sum(queries * k_new.astype(jnp.float32).reshape(REQUESTS, HEADS, HEAD_DIM), axis=-1)) * scale
    page_top = lax.optimization_barrier(jnp.max(scores, axis=-1))
    request_top = jax.ops.segment_max(page_top, page_owner, num_segments=REQUESTS)
    top = jnp.maximum(request_top, own)
    weights = jnp.exp(scores - jnp.take(top, page_owner, axis=0)[:, :, None])
    page_sum = lax.optimization_barrier(jnp.sum(weights, axis=-1))
    page_acc = jnp.einsum('phj,pjhd->phd', weights, values)
    own_weight = jnp.exp(own - top)
    total = jax.ops.segment_sum(page_sum, page_owner, num_segments=REQUESTS) + own_weight
    acc = jax.ops.segment_sum(page_acc, page_owner, num_segments=REQUESTS)
    acc = acc + own_weight[:, :, None] * v_new.astype(jnp.float32).reshape(REQUESTS, HEADS, HEAD_DIM)
    attended = (acc / total[:, :, None]).reshape(REQUESTS, HEADS * HEAD_DIM).astype(jnp.bfloat16)
    attn_out = jnp.dot(attended, out_weight, preferred_element_type=jnp.float32).astype(jnp.bfloat16)
    resid = stream.astype(jnp.float32) + attn_out.astype(jnp.float32)
    normed = resid * lax.rsqrt(lax.optimization_barrier(jnp.mean(resid * resid, axis=-1, keepdims=True)) + 1e-05) * norm_gain.astype(jnp.float32)
    normed = normed.astype(jnp.bfloat16)
    gate_all = w_gate.reshape(EXPERTS, SLICES, D, FF_SLICE).transpose(0, 2, 1, 3).reshape(EXPERTS, D, FF)
    up_all = w_up.reshape(EXPERTS, SLICES, D, FF_SLICE).transpose(0, 2, 1, 3).reshape(EXPERTS, D, FF)
    down_all = w_down.reshape(EXPERTS, FF, D)
    expert_ids = jnp.arange(EXPERTS, dtype=jnp.int32)
    chosen = jnp.zeros((REQUESTS, EXPERTS), jnp.int32)
    coef = jnp.zeros((REQUESTS, EXPERTS), jnp.float32)
    for route in range(TOP):
        match = routes[:, route][:, None] == expert_ids[None, :]
        chosen = chosen + match.astype(jnp.int32)
        coef = coef + jnp.where(match, route_weight[:, route][:, None], jnp.float32(0.0))
    load = N_SEQ * CAP

    def step(carry, pieces):
        gate_w, up_w, down_w, picked_col, coef_col = pieces
        count = jnp.sum(picked_col)
        picked = jnp.nonzero(picked_col == 1, size=load, fill_value=0)[0].astype(jnp.int32)
        rows = jnp.take(normed, picked, axis=0)
        gate = jnp.dot(rows, gate_w, preferred_element_type=jnp.float32)
        up = jnp.dot(rows, up_w, preferred_element_type=jnp.float32)
        hidden = (jax.nn.silu(gate) * up).astype(jnp.bfloat16)
        out = jnp.dot(hidden, down_w, preferred_element_type=jnp.float32)
        live = jnp.arange(load, dtype=jnp.int32) < count
        factor = jnp.where(live, jnp.take(coef_col, picked, axis=0), jnp.float32(0.0))
        return (carry.at[picked].add(factor[:, None] * out), None)
    moe, _ = lax.scan(step, jnp.zeros((REQUESTS, D), jnp.float32), (gate_all, up_all, down_all, chosen.T, coef.T))
    return (attn_out, moe.astype(jnp.bfloat16))
```

```python
import functools
import math

import jax
import jax.numpy as jnp
from jax import lax
from jax.experimental import pallas as pl
from jax.experimental.pallas import tpu as pltpu
from jax.sharding import PartitionSpec as P

HEAD_DIM = 64
EXPERTS = 8
CAP = 2


low_value = -1e30
eps = 1e-05


def per_device(
    stream,
    new_query,
    k_new,
    v_new,
    k_cache,
    v_cache,
    page_owner,
    page_fill,
    out_weight,
    norm_gain,
    routes,
    route_weight,
    w_gate,
    w_up,
    w_down,
):
    seq_count = lax.axis_size("seq")
    seq_rank = lax.axis_index("seq")
    tensor_rank = lax.axis_index("tensor")
    req_dev = stream.shape[0]
    requests = req_dev * seq_count
    width = new_query.shape[1]
    heads_dev = width // HEAD_DIM
    pages_dev = k_cache.shape[0]
    page_len = k_cache.shape[1]
    model_width = stream.shape[1]
    quarter = model_width // lax.axis_size("tensor")
    scale = 1.0 / math.sqrt(HEAD_DIM)
    local_owner = lax.dynamic_slice_in_dim(page_owner, seq_rank * pages_dev, pages_dev, 0)
    all_queries = lax.all_gather(new_query, "seq", axis=0, tiled=True)
    page_queries = jnp.take(all_queries, local_owner, axis=0).reshape(
        pages_dev, heads_dev, HEAD_DIM
    )
    keys = k_cache.reshape(pages_dev, page_len, heads_dev, HEAD_DIM)
    values = v_cache.reshape(pages_dev, page_len, heads_dev, HEAD_DIM).astype(jnp.float32)
    scores = (
        jnp.einsum("phd,pjhd->phj", page_queries, keys, preferred_element_type=jnp.float32) * scale
    )
    valid = lax.broadcasted_iota(jnp.int32, (pages_dev, page_len), 1) < page_fill[:, None]
    scores = jnp.where(valid[:, None, :], scores, low_value)
    page_top = jnp.max(scores, axis=2)
    weights = jnp.exp(scores - page_top[:, :, None])
    page_sum = jnp.sum(weights, axis=2)
    page_acc = jnp.einsum("phj,pjhd->phd", weights, values, precision=lax.Precision.HIGHEST)
    resident_query_rows = new_query.reshape(req_dev, heads_dev, HEAD_DIM)
    own_keys = k_new.reshape(req_dev, heads_dev, HEAD_DIM)
    own_score = (
        jnp.einsum("rhd,rhd->rh", resident_query_rows, own_keys, preferred_element_type=jnp.float32)
        * scale
    )
    own_values = v_new.reshape(req_dev, heads_dev, HEAD_DIM).astype(jnp.float32)
    home_start = seq_rank * req_dev
    request_ids = lax.broadcasted_iota(jnp.int32, (pages_dev, requests), 1)
    owner_hot = local_owner[:, None] == request_ids
    dense_top = jnp.max(jnp.where(owner_hot[:, :, None], page_top[:, None, :], low_value), axis=0)
    local_top_maximum = jnp.maximum(
        lax.dynamic_slice_in_dim(dense_top, home_start, req_dev, 0), own_score
    )
    dense_top = lax.dynamic_update_slice_in_dim(dense_top, local_top_maximum, home_start, 0)
    global_top = lax.pmax(dense_top, "seq")
    factor = jnp.exp(page_top - jnp.take(global_top, local_owner, axis=0))
    hot = owner_hot.astype(jnp.float32)
    dense_sum = jnp.einsum("pr,ph->rh", hot, page_sum * factor, precision=lax.Precision.HIGHEST)
    dense_acc = jnp.einsum(
        "pr,phd->rhd", hot, page_acc * factor[:, :, None], precision=lax.Precision.HIGHEST
    )
    own_factor = jnp.exp(own_score - lax.dynamic_slice_in_dim(global_top, home_start, req_dev, 0))
    home_sum = lax.dynamic_slice_in_dim(dense_sum, home_start, req_dev, 0) + own_factor
    dense_sum = lax.dynamic_update_slice_in_dim(dense_sum, home_sum, home_start, 0)
    home_acc = (
        lax.dynamic_slice_in_dim(dense_acc, home_start, req_dev, 0)
        + own_factor[:, :, None] * own_values
    )
    dense_acc = lax.dynamic_update_slice_in_dim(dense_acc, home_acc, home_start, 0)
    merged_sum, merged_acc = lax.psum((dense_sum, dense_acc), "seq")
    attention = merged_acc / merged_sum[:, :, None]
    attended = attention.reshape(requests, width).astype(jnp.bfloat16)
    projected_part = jnp.dot(attended, out_weight, preferred_element_type=jnp.float32)
    home_part = lax.all_to_all(projected_part, "seq", split_axis=0, concat_axis=1, tiled=True)
    attn_full = lax.psum(home_part, "tensor")
    attention_rounded = attn_full.astype(jnp.bfloat16)
    attn_out = lax.dynamic_slice_in_dim(attention_rounded, tensor_rank * quarter, quarter, 1)
    resid = stream.astype(jnp.float32) + attention_rounded.astype(jnp.float32)
    normed = resid * lax.rsqrt(jnp.mean(resid * resid, axis=-1, keepdims=True) + eps) * norm_gain
    normed = normed.astype(jnp.bfloat16)
    my_columns = lax.dynamic_slice_in_dim(normed, tensor_rank * quarter, quarter, 1)
    expert_ids = lax.broadcasted_iota(jnp.int32, (req_dev, EXPERTS), 1)
    chosen = jnp.zeros((req_dev, EXPERTS), jnp.int32)
    coef = jnp.zeros((req_dev, EXPERTS), jnp.float32)
    for route in range(routes.shape[1]):
        match = routes[:, route : route + 1] == expert_ids
        chosen = chosen + match.astype(jnp.int32)
        coef = coef + jnp.where(match, route_weight[:, route : route + 1], 0.0)
    rank = jnp.cumsum(chosen, axis=0) - chosen
    slot_ids = lax.broadcasted_iota(jnp.int32, (EXPERTS, CAP, req_dev), 1)
    placed = (chosen.T[:, None, :] == 1) & (rank.T[:, None, :] == slot_ids)
    slices = seq_count // EXPERTS
    placed_dest = jnp.repeat(placed, slices, axis=0)
    send = jnp.einsum(
        "lwb,bo->lwo",
        placed_dest.astype(jnp.bfloat16),
        my_columns,
        preferred_element_type=jnp.float32,
    ).astype(jnp.bfloat16)
    rows = lax.all_to_all(send, "seq", split_axis=0, concat_axis=0, tiled=True)
    count_src, count_items, columns = rows.shape
    flat = rows.reshape(count_src * count_items, columns)
    gate_part = jnp.dot(flat, w_gate[0], preferred_element_type=jnp.float32)
    up_part = jnp.dot(flat, w_up[0], preferred_element_type=jnp.float32)
    stacked = jnp.stack([gate_part, up_part])
    summed = lax.psum(stacked, "tensor")
    hidden = (jax.nn.silu(summed[0]) * summed[1]).astype(jnp.bfloat16)
    down = jnp.dot(hidden, w_down[0], preferred_element_type=jnp.float32)
    expert_out = down.reshape(count_src, count_items, down.shape[1])
    returned_output = lax.all_to_all(
        expert_out.astype(jnp.bfloat16), "seq", split_axis=0, concat_axis=0, tiled=True
    ).astype(expert_out.dtype)
    weighted_output_rows = (
        placed_dest.astype(jnp.float32) * jnp.repeat(coef.T, slices, axis=0)[:, None, :]
    )
    mixture_expert_partial = jnp.einsum(
        "ubp,ubr->pr", weighted_output_rows, returned_output, precision=lax.Precision.HIGHEST
    )
    return (attn_out, mixture_expert_partial.astype(jnp.bfloat16))

LANES = 128
MESH = pl.DeviceIdType.MESH
HIGH = lax.Precision.HIGHEST
f32 = jnp.float32
bf16 = jnp.bfloat16


def iota(shape, dim):
    return lax.broadcasted_iota(jnp.int32, shape, dim)


def dot(a, b, precision=None):
    return jnp.dot(a, b, preferred_element_type=f32, precision=precision)


def packed(x, strips):
    gap = strips * LANES - x.shape[1]
    if gap:
        x = jnp.concatenate([x, jnp.zeros((x.shape[0], gap), x.dtype)], axis=1)
    return [x[:, j * LANES : (j + 1) * LANES] for j in range(strips)]


def layer_kernel(
    n_seq,
    n_tensor,
    owner_ref,
    fill_ref,
    routes_ref,
    rw_ref,
    q_ref,
    kn_ref,
    vn_ref,
    stream_ref,
    gain_ref,
    kc_hbm,
    vc_hbm,
    ow_hbm,
    wg_hbm,
    wu_hbm,
    wd_hbm,
    attn_ref,
    moe_ref,
    kc,
    vc,
    ow,
    wg,
    wu,
    wd,
    qbuf,
    ebuf,
    bbuf,
    psend,
    precv,
    ssq,
    gsend,
    grecv,
    hid,
    osend,
    orecv,
    lsem,
    qs,
    qr,
    es,
    er,
    bs,
    br,
    ps,
    pr,
    ss,
    sr,
    gs,
    gr,
    hs,
    hr,
    os_,
    or_,
):
    s = lax.axis_index("seq")
    t = lax.axis_index("tensor")
    req, width = q_ref.shape
    requests = req * n_seq
    pages, slots, _ = kc.shape
    heads = width // HEAD_DIM
    strips = -(-width // LANES)
    cols = ow.shape[1]
    ff = wg_hbm.shape[2]
    chunk = hid.shape[2]
    rows = n_seq * CAP
    hp = 16

    loads = [
        pltpu.make_async_copy(a, b, lsem.at[i])
        for i, (a, b) in enumerate(
            [
                (kc_hbm, kc),
                (vc_hbm, vc),
                (ow_hbm, ow),
                (wg_hbm.at[0], wg.at[:, 0:ff]),
                (wu_hbm.at[0], wu.at[:, 0:ff]),
                (wd_hbm.at[0], wd.at[0:ff, :]),
            ]
        )
    ]
    for load in loads:
        load.start()

    barrier = pltpu.get_barrier_semaphore()
    total_devices = n_seq * n_tensor
    me = s * n_tensor + t

    def greet(i, carry):
        other = lax.rem(me + i, total_devices)
        pl.semaphore_signal(
            barrier,
            inc=1,
            device_id=(other // n_tensor, lax.rem(other, n_tensor)),
            device_id_type=MESH,
        )
        return carry

    lax.fori_loop(1, total_devices, greet, 0)

    def seq_copy(src, dst, send, recv, k, slot):
        peer = lax.rem(s + k, n_seq)
        return pltpu.make_async_remote_copy(
            src_ref=src,
            dst_ref=dst,
            send_sem=send.at[k],
            recv_sem=recv.at[slot],
            device_id=(peer, t),
            device_id_type=MESH,
        )

    def gather_start(buf, send, recv):
        for k in range(1, n_seq):
            seq_copy(buf.at[s], buf.at[s], send, recv, k, s).start()

    def gather_wait(buf, send, recv):
        for k in range(1, n_seq):
            src = lax.rem(s + k, n_seq)
            seq_copy(buf.at[src], buf.at[src], send, recv, k, src).wait_recv()

    def gather_sent(buf, send, recv):
        for k in range(1, n_seq):
            seq_copy(buf.at[s], buf.at[s], send, recv, k, s).wait_send()

    q = q_ref[...].astype(f32)
    lane_row = iota((1, LANES), 1)
    route_rows = []
    for i in range(2):
        row = jnp.zeros((1, LANES), f32)
        for r in range(req):
            value = jnp.full((1, LANES), routes_ref[r, i], jnp.int32).astype(f32)
            row = jnp.where(lane_row == s * req + r, value, row)
        route_rows.append(row)
    rest = qbuf.shape[1] - strips * req - 2
    qbuf[s] = jnp.concatenate(
        packed(q, strips) + route_rows + [jnp.zeros((rest, LANES), f32)], axis=0
    ).astype(bf16)

    stream = stream_ref[...].astype(f32)
    part = stream[:, 0:width]
    gain = gain_ref[:, 0:width]
    for i in range(1, n_tensor):
        here = t == i
        part = jnp.where(here, stream[:, i * width : (i + 1) * width], part)
        gain = jnp.where(here, gain_ref[:, i * width : (i + 1) * width], gain)
    vn = vn_ref[...].astype(f32)
    rest = ebuf.shape[1] - 2 * strips * req
    ebuf[s] = jnp.concatenate(
        packed(part, strips) + packed(vn, strips) + [jnp.zeros((rest, LANES), f32)], axis=0
    ).astype(bf16)

    pl.semaphore_wait(barrier, total_devices - 1)
    gather_start(qbuf, qs, qr)
    gather_start(ebuf, es, er)

    wg[:, ff:] = jnp.zeros((wg.shape[0], wg.shape[1] - ff), bf16)
    wu[:, ff:] = jnp.zeros((wu.shape[0], wu.shape[1] - ff), bf16)
    wd[ff:, :] = jnp.zeros((wd.shape[0] - ff, wd.shape[1]), bf16)

    head_of = iota((width, LANES), 0) - HEAD_DIM * (iota((width, LANES), 1) - 16)
    to_own = ((head_of >= 0) & (head_of < HEAD_DIM)).astype(f32)
    from_head = iota((LANES, width), 1) - HEAD_DIM * iota((LANES, width), 0)
    spread = ((from_head >= 0) & (from_head < HEAD_DIM)).astype(f32)
    product = jnp.concatenate(
        [q * kn_ref[...].astype(f32), jnp.zeros((8 - req, width), f32)], axis=0
    )
    own_row = dot(product, to_own, HIGH)[0:req] * (1.0 / math.sqrt(HEAD_DIM))

    ph = pages * hp
    sub = iota((ph, 1), 0)
    page_row = sub >> 4
    head_row = sub & 15
    target = jnp.zeros((ph, 1), jnp.int32)
    high = jnp.zeros((ph, 1), jnp.int32)
    for p in range(pages):
        owner = owner_ref[s * pages + p]
        home = lax.div(owner, req)
        target = jnp.where(
            page_row == p, home * qbuf.shape[1] + (owner - home * req), target
        )
        high = jnp.where(page_row == p, p * slots + fill_ref[p], high)
    lane = iota((ph, pages * slots), 1)
    valid = (lane >= page_row * slots) & (lane < high)
    channel = iota((ph, width), 1) - HEAD_DIM * head_row
    head_mask = ((channel >= 0) & (channel < HEAD_DIM)).astype(f32)
    qlane = iota((ph, n_seq * qbuf.shape[1]), 1)
    picks = [(qlane == target + req * j).astype(bf16) for j in range(strips)]

    all_pages = pages * n_seq
    sub_r = iota((requests, LANES), 0)
    lane_r = iota((requests, LANES), 1)
    hot_pr = jnp.zeros((requests, LANES), f32)
    hot_rp = jnp.zeros((requests, LANES), f32)
    for p in range(all_pages):
        owner = owner_ref[p]
        hot_pr = jnp.where((sub_r == p) & (lane_r == owner), 1.0, hot_pr)
        hot_rp = jnp.where((sub_r == owner) & (lane_r == p), 1.0, hot_rp)
    hot_pr = hot_pr[:, 0:requests]
    hot_rp = hot_rp[:, 0:all_pages]

    loads[0].wait()
    gather_wait(qbuf, qs, qr)
    queries = qbuf[...].reshape(n_seq * qbuf.shape[1], LANES)
    page_q = jnp.concatenate([dot(pick, queries) for pick in picks], axis=1)[:, 0:width]
    page_q = (page_q * head_mask).astype(bf16)
    keys = kc[...].reshape(pages * slots, width)
    scores = lax.dot_general(
        page_q, keys, (((1,), (1,)), ((), ())), preferred_element_type=f32
    ) * (1.0 / math.sqrt(HEAD_DIM))
    scores = jnp.where(valid, scores, low_value)
    page_top = jnp.max(scores, axis=1, keepdims=True)
    weights = jnp.exp(scores - page_top)
    page_sum = jnp.sum(weights, axis=1, keepdims=True)
    loads[1].wait()
    values = vc[...].reshape(pages * slots, width)
    page_acc = dot(weights.astype(bf16), values) * (head_mask * (1.0 / page_sum))
    page_acc = jnp.sum(page_acc.reshape(pages, hp, width), axis=1)
    level = page_top + jnp.log(page_sum)
    level = jnp.where(iota((ph, LANES), 1) == head_row, level, 0.0)
    level = jnp.sum(level.reshape(pages, hp, LANES), axis=1)
    bbuf[s] = jnp.concatenate(packed(page_acc, strips) + [level + own_row], axis=0)
    gather_start(bbuf, bs, br)

    routed = qbuf[0, 16:32, :].astype(f32)
    for i in range(1, n_seq):
        routed = routed + qbuf[i, 16:32, :].astype(f32)
    first = strips * req - 16
    expert = jnp.full((1, LANES), s, jnp.int32).astype(f32)
    chosen = jnp.where(
        (routed[first : first + 1] == expert) | (routed[first + 1 : first + 2] == expert),
        1.0,
        0.0,
    )
    lane_1 = iota((1, LANES), 1)
    chosen = jnp.where(lane_1 < requests, chosen, 0.0)
    before_a = iota((LANES, LANES), 0)
    before_b = iota((LANES, LANES), 1)
    before = ((before_a < before_b) & ((before_a >> 2) == (before_b >> 2))).astype(bf16)
    rank = dot(jnp.broadcast_to(chosen, (16, LANES)).astype(bf16), before)
    slot_row = iota((rows, LANES), 0)
    slot_lane = iota((rows, LANES), 1)
    place = jnp.where(
        ((slot_lane >> 2) == (slot_row >> 1))
        & (rank == (slot_row & 1).astype(f32)),
        jnp.broadcast_to(chosen, (rows, LANES)),
        0.0,
    )[:, 0:requests].astype(bf16)

    home_row = iota((8, requests), 0)
    at_home = ((iota((8, requests), 1) == home_row + s * req) & (home_row < req)).astype(bf16)

    gather_wait(ebuf, es, er)

    def unpacked(buf, offset, kind):
        return jnp.concatenate(
            [
                jnp.concatenate(
                    [
                        buf[i].astype(f32)[offset + j * req : offset + (j + 1) * req]
                        for i in range(n_seq)
                    ],
                    axis=0,
                )
                for j in range(strips)
            ],
            axis=1,
        )[:, 0:width].astype(kind)

    stream_rows = dot(place, unpacked(ebuf, 0, bf16))
    new_values = unpacked(ebuf, strips * req, f32)

    gather_wait(bbuf, bs, br)
    levels = jnp.concatenate([bbuf[i, strips * req :, :] for i in range(n_seq)], axis=0)
    own = jnp.concatenate([levels[:, 16:], levels[:, 0:16]], axis=1)
    top = own
    for p in range(all_pages):
        top = jnp.maximum(top, jnp.where(sub_r == owner_ref[p], levels[p : p + 1], low_value))
    factor = jnp.exp(levels - dot(hot_pr, top, HIGH))
    own_factor = jnp.exp(own - top)
    wide = dot(jnp.concatenate([factor, own_factor], axis=0), spread, HIGH)
    page_wide, own_wide = wide[0:all_pages], wide[all_pages:]
    acc = dot(hot_rp, page_wide * unpacked(bbuf, 0, f32), HIGH) + own_wide * new_values
    total = 1.0 / (dot(hot_rp, factor, HIGH) + own_factor)
    attended = (acc * dot(total, spread, HIGH)).astype(bf16)

    loads[2].wait()
    projected = dot(attended, ow[...])
    psend[...] = jnp.concatenate(
        [projected, jnp.zeros((requests, psend.shape[1] - cols), f32)], axis=1
    ).astype(bf16)
    ratio = n_seq // n_tensor
    column = s // ratio
    pslot = lax.rem(s, ratio) * n_tensor + t

    def part_copy(k):
        return pltpu.make_async_remote_copy(
            src_ref=psend,
            dst_ref=precv.at[pslot],
            send_sem=ps.at[k],
            recv_sem=pr.at[pslot],
            device_id=(lax.rem(s + k, n_seq), column),
            device_id_type=MESH,
        )

    def self_part():
        return pltpu.make_async_copy(psend, precv.at[pslot], pr.at[pslot])

    for k in range(1, n_seq):
        part_copy(k).start()

    @pl.when(column != t)
    def _():
        part_copy(0).start()

    @pl.when(column == t)
    def _():
        self_part().start()

    halves = []
    for half in range(ratio):
        piece = None
        for i in range(n_tensor):
            j = half * n_tensor + i
            pltpu.make_async_copy(psend, precv.at[j], pr.at[j]).wait()
            term = precv[j].astype(f32)
            piece = term if piece is None else piece + term
        halves.append(piece[:, 0:cols])
    attn = jnp.concatenate(halves, axis=1).astype(bf16)

    resid = stream_rows + dot(place, attn)
    ssq[0] = jnp.broadcast_to(jnp.sum(resid * resid, axis=1, keepdims=True), (rows, LANES))
    x = (resid * gain).astype(bf16)

    low = lax.rem(t, 2)
    partners = [t, t + 1 - 2 * low, lax.rem(t + 2, 4), 3 - t]

    def tensor_copy(src, dst, send, recv, k, slot):
        return pltpu.make_async_remote_copy(
            src_ref=src,
            dst_ref=dst,
            send_sem=send.at[k],
            recv_sem=recv.at[slot],
            device_id=(s, partners[k]),
            device_id_type=MESH,
        )

    ssq_copies = [None] + [
        tensor_copy(ssq.at[0], ssq.at[k], ss, sr, k, k) for k in range(1, n_tensor)
    ]
    gate_copies = [None] + [
        tensor_copy(gsend.at[k], grecv.at[k], gs, gr, k, k) for k in range(1, n_tensor)
    ]
    for k in range(1, n_tensor):
        ssq_copies[k].start()
    loads[3].wait()
    loads[4].wait()
    for k in (2, 3, 1, 0):
        span = pl.ds(pl.multiple_of(partners[k] * chunk, LANES), chunk)
        gate = dot(x, wg[:, span])
        up = dot(x, wu[:, span])
        if k:
            gsend[k, 0] = gate.astype(bf16)
            gsend[k, 1] = up.astype(bf16)
            gate_copies[k].start()

    attn_ref[...] = dot(at_home, attn)[0:req].astype(bf16)
    mean = ssq[0]
    for k in (1, 2, 3):
        ssq_copies[k].wait_recv()
        mean = mean + ssq[k]
    root = lax.rsqrt(mean[:, 0:1] * (1.0 / (width * n_tensor)) + eps)
    for k in (1, 2, 3):
        gate_copies[k].wait_recv()
        gate = gate + grecv[k, 0].astype(f32)
        up = up + grecv[k, 1].astype(f32)
    gate = gate * root
    up = up * root
    hid[0] = (gate / (1.0 + jnp.exp(-gate)) * up).astype(bf16)
    hid_copies = [None] + [
        tensor_copy(hid.at[0], hid.at[k], hs, hr, k, k) for k in range(1, n_tensor)
    ]
    for k in (2, 3, 1):
        hid_copies[k].start()

    wsub = iota((8 * strips, LANES), 0)
    wlane = iota((8 * strips, LANES), 1) - CAP * (wsub >> 3)
    mix = jnp.zeros((8 * strips, LANES), f32)
    for r in range(req):
        for i in range(2):
            e = routes_ref[r, i]
            taken = jnp.int32(0)
            for r2 in range(r):
                for i2 in range(2):
                    taken = taken + (routes_ref[r2, i2] == e).astype(jnp.int32)
            mix = jnp.where(
                ((wsub & 7) == r) & (wlane == e * 16 + taken), rw_ref[r, i], mix
            )

    loads[5].wait()
    out = None
    for k in (0, 1, 2, 3):
        if k:
            hid_copies[k].wait_recv()
        span = pl.ds(pl.multiple_of(partners[k] * chunk, LANES), chunk)
        term = dot(hid[k], wd[span, :])
        out = term if out is None else out + term

    tiles = packed(out, strips)
    fill = jnp.zeros((16 - CAP * strips, LANES), f32)
    for d in range(n_seq):
        osend[d] = jnp.concatenate(
            [tile[CAP * d : CAP * (d + 1)] for tile in tiles] + [fill], axis=0
        ).astype(bf16)
    for k in range(1, n_seq):
        peer = lax.rem(s + k, n_seq)
        seq_copy(osend.at[peer], orecv.at[s], os_, or_, k, s).start()
    orecv[s] = osend[s]
    for k in range(1, n_seq):
        peer = lax.rem(s + k, n_seq)
        seq_copy(osend.at[peer], orecv.at[peer], os_, or_, k, peer).wait_recv()
    returned = orecv[...].astype(f32).reshape(n_seq * 16, LANES)
    mixed = dot(mix, returned, HIGH)
    moe = jnp.concatenate([mixed[8 * j : 8 * j + req] for j in range(strips)], axis=1)
    moe_ref[...] = moe[:, 0:width].astype(bf16)

    gather_sent(qbuf, qs, qr)
    gather_sent(ebuf, es, er)
    gather_sent(bbuf, bs, br)
    for k in range(1, n_seq):
        part_copy(k).wait_send()

    @pl.when(column != t)
    def _():
        part_copy(0).wait_send()

    for k in range(1, n_tensor):
        ssq_copies[k].wait_send()
        gate_copies[k].wait_send()
        hid_copies[k].wait_send()
    for k in range(1, n_seq):
        peer = lax.rem(s + k, n_seq)
        seq_copy(osend.at[peer], orecv.at[s], os_, or_, k, s).wait_send()


def one_kernel(n_seq, n_tensor, *args):
    (
        stream,
        new_query,
        k_new,
        v_new,
        k_cache,
        v_cache,
        page_owner,
        page_fill,
        out_weight,
        norm_gain,
        routes,
        route_weight,
        w_gate,
        w_up,
        w_down,
    ) = args
    req, width = new_query.shape
    ff = w_gate.shape[2]
    cols = out_weight.shape[1]
    requests = req * n_seq
    strips = -(-width // LANES)
    chunk = -(-ff // (n_tensor * LANES)) * LANES
    rows = n_seq * CAP
    smem = pl.BlockSpec(memory_space=pltpu.SMEM)
    vmem = pl.BlockSpec(memory_space=pltpu.VMEM)
    hbm = pl.BlockSpec(memory_space=pl.ANY)
    dma = pltpu.SemaphoreType.DMA
    out = jax.ShapeDtypeStruct((req, width), bf16)
    return pl.pallas_call(
        functools.partial(layer_kernel, n_seq, n_tensor),
        out_shape=(out, out),
        in_specs=[smem] * 4 + [vmem] * 5 + [hbm] * 6,
        out_specs=(vmem, vmem),
        scratch_shapes=[
            pltpu.VMEM(k_cache.shape, bf16),
            pltpu.VMEM(v_cache.shape, bf16),
            pltpu.VMEM(out_weight.shape, bf16),
            pltpu.VMEM((width, chunk * n_tensor), bf16),
            pltpu.VMEM((width, chunk * n_tensor), bf16),
            pltpu.VMEM((chunk * n_tensor, width), bf16),
            pltpu.VMEM((n_seq, 32, LANES), bf16),
            pltpu.VMEM((n_seq, 48, LANES), bf16),
            pltpu.VMEM((n_seq, 24, LANES), f32),
            pltpu.VMEM((requests, -(-cols // LANES) * LANES), bf16),
            pltpu.VMEM((n_seq, requests, -(-cols // LANES) * LANES), bf16),
            pltpu.VMEM((n_tensor, rows, LANES), f32),
            pltpu.VMEM((n_tensor, 2, rows, chunk), bf16),
            pltpu.VMEM((n_tensor, 2, rows, chunk), bf16),
            pltpu.VMEM((n_tensor, rows, chunk), bf16),
            pltpu.VMEM((n_seq, 16, LANES), bf16),
            pltpu.VMEM((n_seq, 16, LANES), bf16),
            dma((6,)),
        ]
        + [dma((n_seq,))] * 8
        + [dma((n_tensor,))] * 6
        + [dma((n_seq,))] * 2,
        compiler_params=pltpu.CompilerParams(
            collective_id=0, has_side_effects=True, vmem_limit_bytes=56 * 1024 * 1024
        ),
        name="layer",
    )(
        page_owner,
        page_fill,
        routes,
        route_weight,
        new_query,
        k_new,
        v_new,
        stream,
        norm_gain.reshape(1, -1),
        k_cache,
        v_cache,
        out_weight,
        w_gate,
        w_up,
        w_down,
    )


def fits_one_kernel(n_seq, n_tensor, args):
    req, width = args[1].shape
    pages = args[4].shape[0]
    strips = -(-width // LANES)
    return (
        n_seq == EXPERTS
        and n_tensor == 4
        and req == 4
        and pages == 4
        and strips == 5
        and width % HEAD_DIM == 0
        and width // HEAD_DIM <= 16
        and args[8].shape[1] * (n_seq // n_tensor) == width
    )


def either(n_seq, n_tensor, *args):
    if fits_one_kernel(n_seq, n_tensor, args):
        return one_kernel(n_seq, n_tensor, *args)
    return per_device(*args)


def solution(mesh):
    in_specs = (
        P("seq", None),
        P("seq", "tensor"),
        P("seq", "tensor"),
        P("seq", "tensor"),
        P("seq", None, "tensor"),
        P("seq", None, "tensor"),
        P(),
        P("seq"),
        P("tensor", "seq"),
        P(),
        P("seq", None),
        P("seq", None),
        P("seq", "tensor", None),
        P("seq", "tensor", None),
        P("seq", None, "tensor"),
    )
    out_specs = (P("seq", "tensor"), P("seq", "tensor"))
    return jax.shard_map(
        functools.partial(either, mesh.shape["seq"], mesh.shape["tensor"]), mesh=mesh, in_specs=in_specs, out_specs=out_specs, check_vma=False
    )
```

```python
import functools
import math

import jax
import jax.numpy as jnp
from jax import lax
from jax.experimental import pallas as pl
from jax.experimental.pallas import tpu as pltpu
from jax.sharding import PartitionSpec as P

HEAD_DIM = 64
EXPERTS = 8
CAP = 2


low_value = -1e30
eps = 1e-05


def per_device(
    stream,
    new_query,
    k_new,
    v_new,
    k_cache,
    v_cache,
    page_owner,
    page_fill,
    out_weight,
    norm_gain,
    routes,
    route_weight,
    w_gate,
    w_up,
    w_down,
):
    seq_count = lax.axis_size("seq")
    seq_rank = lax.axis_index("seq")
    tensor_rank = lax.axis_index("tensor")
    req_dev = stream.shape[0]
    requests = req_dev * seq_count
    width = new_query.shape[1]
    heads_dev = width // HEAD_DIM
    pages_dev = k_cache.shape[0]
    page_len = k_cache.shape[1]
    model_width = stream.shape[1]
    quarter = model_width // lax.axis_size("tensor")
    scale = 1.0 / math.sqrt(HEAD_DIM)
    local_owner = lax.dynamic_slice_in_dim(page_owner, seq_rank * pages_dev, pages_dev, 0)
    all_queries = lax.all_gather(new_query, "seq", axis=0, tiled=True)
    page_queries = jnp.take(all_queries, local_owner, axis=0).reshape(
        pages_dev, heads_dev, HEAD_DIM
    )
    keys = k_cache.reshape(pages_dev, page_len, heads_dev, HEAD_DIM)
    values = v_cache.reshape(pages_dev, page_len, heads_dev, HEAD_DIM).astype(jnp.float32)
    scores = (
        jnp.einsum("phd,pjhd->phj", page_queries, keys, preferred_element_type=jnp.float32) * scale
    )
    valid = lax.broadcasted_iota(jnp.int32, (pages_dev, page_len), 1) < page_fill[:, None]
    scores = jnp.where(valid[:, None, :], scores, low_value)
    page_top = jnp.max(scores, axis=2)
    weights = jnp.exp(scores - page_top[:, :, None])
    page_sum = jnp.sum(weights, axis=2)
    page_acc = jnp.einsum("phj,pjhd->phd", weights, values, precision=lax.Precision.HIGHEST)
    resident_query_rows = new_query.reshape(req_dev, heads_dev, HEAD_DIM)
    own_keys = k_new.reshape(req_dev, heads_dev, HEAD_DIM)
    own_score = (
        jnp.einsum("rhd,rhd->rh", resident_query_rows, own_keys, preferred_element_type=jnp.float32)
        * scale
    )
    own_values = v_new.reshape(req_dev, heads_dev, HEAD_DIM).astype(jnp.float32)
    home_start = seq_rank * req_dev
    request_ids = lax.broadcasted_iota(jnp.int32, (pages_dev, requests), 1)
    owner_hot = local_owner[:, None] == request_ids
    dense_top = jnp.max(jnp.where(owner_hot[:, :, None], page_top[:, None, :], low_value), axis=0)
    local_top_maximum = jnp.maximum(
        lax.dynamic_slice_in_dim(dense_top, home_start, req_dev, 0), own_score
    )
    dense_top = lax.dynamic_update_slice_in_dim(dense_top, local_top_maximum, home_start, 0)
    global_top = lax.pmax(dense_top, "seq")
    factor = jnp.exp(page_top - jnp.take(global_top, local_owner, axis=0))
    hot = owner_hot.astype(jnp.float32)
    dense_sum = jnp.einsum("pr,ph->rh", hot, page_sum * factor, precision=lax.Precision.HIGHEST)
    dense_acc = jnp.einsum(
        "pr,phd->rhd", hot, page_acc * factor[:, :, None], precision=lax.Precision.HIGHEST
    )
    own_factor = jnp.exp(own_score - lax.dynamic_slice_in_dim(global_top, home_start, req_dev, 0))
    home_sum = lax.dynamic_slice_in_dim(dense_sum, home_start, req_dev, 0) + own_factor
    dense_sum = lax.dynamic_update_slice_in_dim(dense_sum, home_sum, home_start, 0)
    home_acc = (
        lax.dynamic_slice_in_dim(dense_acc, home_start, req_dev, 0)
        + own_factor[:, :, None] * own_values
    )
    dense_acc = lax.dynamic_update_slice_in_dim(dense_acc, home_acc, home_start, 0)
    merged_sum, merged_acc = lax.psum((dense_sum, dense_acc), "seq")
    attention = merged_acc / merged_sum[:, :, None]
    attended = attention.reshape(requests, width).astype(jnp.bfloat16)
    projected_part = jnp.dot(attended, out_weight, preferred_element_type=jnp.float32)
    home_part = lax.all_to_all(projected_part, "seq", split_axis=0, concat_axis=1, tiled=True)
    attn_full = lax.psum(home_part, "tensor")
    attention_rounded = attn_full.astype(jnp.bfloat16)
    attn_out = lax.dynamic_slice_in_dim(attention_rounded, tensor_rank * quarter, quarter, 1)
    resid = stream.astype(jnp.float32) + attention_rounded.astype(jnp.float32)
    normed = resid * lax.rsqrt(jnp.mean(resid * resid, axis=-1, keepdims=True) + eps) * norm_gain
    normed = normed.astype(jnp.bfloat16)
    my_columns = lax.dynamic_slice_in_dim(normed, tensor_rank * quarter, quarter, 1)
    expert_ids = lax.broadcasted_iota(jnp.int32, (req_dev, EXPERTS), 1)
    chosen = jnp.zeros((req_dev, EXPERTS), jnp.int32)
    coef = jnp.zeros((req_dev, EXPERTS), jnp.float32)
    for route in range(routes.shape[1]):
        match = routes[:, route : route + 1] == expert_ids
        chosen = chosen + match.astype(jnp.int32)
        coef = coef + jnp.where(match, route_weight[:, route : route + 1], 0.0)
    rank = jnp.cumsum(chosen, axis=0) - chosen
    slot_ids = lax.broadcasted_iota(jnp.int32, (EXPERTS, CAP, req_dev), 1)
    placed = (chosen.T[:, None, :] == 1) & (rank.T[:, None, :] == slot_ids)
    slices = seq_count // EXPERTS
    placed_dest = jnp.repeat(placed, slices, axis=0)
    send = jnp.einsum(
        "lwb,bo->lwo",
        placed_dest.astype(jnp.bfloat16),
        my_columns,
        preferred_element_type=jnp.float32,
    ).astype(jnp.bfloat16)
    rows = lax.all_to_all(send, "seq", split_axis=0, concat_axis=0, tiled=True)
    count_src, count_items, columns = rows.shape
    flat = rows.reshape(count_src * count_items, columns)
    gate_part = jnp.dot(flat, w_gate[0], preferred_element_type=jnp.float32)
    up_part = jnp.dot(flat, w_up[0], preferred_element_type=jnp.float32)
    stacked = jnp.stack([gate_part, up_part])
    summed = lax.psum(stacked, "tensor")
    hidden = (jax.nn.silu(summed[0]) * summed[1]).astype(jnp.bfloat16)
    down = jnp.dot(hidden, w_down[0], preferred_element_type=jnp.float32)
    expert_out = down.reshape(count_src, count_items, down.shape[1])
    returned_output = lax.all_to_all(
        expert_out.astype(jnp.bfloat16), "seq", split_axis=0, concat_axis=0, tiled=True
    ).astype(expert_out.dtype)
    weighted_output_rows = (
        placed_dest.astype(jnp.float32) * jnp.repeat(coef.T, slices, axis=0)[:, None, :]
    )
    mixture_expert_partial = jnp.einsum(
        "ubp,ubr->pr", weighted_output_rows, returned_output, precision=lax.Precision.HIGHEST
    )
    return (attn_out, mixture_expert_partial.astype(jnp.bfloat16))

LANES = 128
MESH = pl.DeviceIdType.MESH
HIGH = lax.Precision.HIGHEST
f32 = jnp.float32
bf16 = jnp.bfloat16


def iota(shape, dim):
    return lax.broadcasted_iota(jnp.int32, shape, dim)


def dot(a, b, precision=None):
    return jnp.dot(a, b, preferred_element_type=f32, precision=precision)


def dot_t(a, b):
    return lax.dot_general(a, b, (((1,), (1,)), ((), ())), preferred_element_type=f32)


def packed(x, strips):
    gap = strips * LANES - x.shape[1]
    if gap:
        x = jnp.concatenate([x, jnp.zeros((x.shape[0], gap), x.dtype)], axis=1)
    return [x[:, j * LANES : (j + 1) * LANES] for j in range(strips)]


def layer_kernel(
    n_seq,
    n_tensor,
    owner_ref,
    fill_ref,
    routes_ref,
    rw_ref,
    q_ref,
    kn_ref,
    vn_ref,
    stream_ref,
    gain_ref,
    kc_hbm,
    vc_hbm,
    ow_hbm,
    wg_hbm,
    wu_hbm,
    wd_hbm,
    out_ref,
    kc,
    vc,
    ow,
    wg,
    wu,
    wd,
    qbuf,
    ebuf,
    bbuf,
    psend,
    precv,
    ssq,
    gsend,
    grecv,
    hid,
    osend,
    orecv,
    lsem,
    qs,
    qr,
    es,
    er,
    bs,
    br,
    ps,
    pr,
    ss,
    sr,
    gs,
    gr,
    hs,
    hr,
    os_,
    or_,
):
    s = lax.axis_index("seq")
    t = lax.axis_index("tensor")
    req, width = q_ref.shape
    requests = req * n_seq
    pages, slots, _ = kc.shape
    heads = width // HEAD_DIM
    strips = -(-width // LANES)
    cols = ow.shape[0]
    ff = wg_hbm.shape[2]
    chunk = hid.shape[2]
    rows = n_seq * CAP
    hp = 16

    loads = [
        pltpu.make_async_copy(a, b, lsem.at[i])
        for i, (a, b) in enumerate(
            [
                (kc_hbm, kc),
                (vc_hbm, vc),
                (ow_hbm, ow),
                (wg_hbm.at[0], wg.at[:, 0:ff]),
                (wu_hbm.at[0], wu.at[:, 0:ff]),
                (wd_hbm.at[0], wd.at[:, 0:ff]),
            ]
        )
    ]
    for load in loads:
        load.start()

    barrier = pltpu.get_barrier_semaphore()
    total_devices = n_seq * n_tensor
    me = s * n_tensor + t

    def greet(i, carry):
        other = lax.rem(me + i, total_devices)
        pl.semaphore_signal(
            barrier,
            inc=1,
            device_id=(other // n_tensor, lax.rem(other, n_tensor)),
            device_id_type=MESH,
        )
        return carry

    lax.fori_loop(1, total_devices, greet, 0)

    def seq_copy(src, dst, send, recv, k, slot):
        peer = lax.rem(s + k, n_seq)
        return pltpu.make_async_remote_copy(
            src_ref=src,
            dst_ref=dst,
            send_sem=send.at[k],
            recv_sem=recv.at[slot],
            device_id=(peer, t),
            device_id_type=MESH,
        )

    def gather_start(buf, send, recv):
        for k in range(1, n_seq):
            seq_copy(buf.at[s], buf.at[s], send, recv, k, s).start()

    def gather_wait(buf, send, recv):
        for k in range(1, n_seq):
            src = lax.rem(s + k, n_seq)
            seq_copy(buf.at[src], buf.at[src], send, recv, k, src).wait_recv()

    def gather_sent(buf, send, recv):
        for k in range(1, n_seq):
            seq_copy(buf.at[s], buf.at[s], send, recv, k, s).wait_send()

    q = q_ref[...].astype(f32)
    lane_row = iota((1, LANES), 1)
    route_rows = []
    for i in range(2):
        row = jnp.zeros((1, LANES), f32)
        for r in range(req):
            value = jnp.full((1, LANES), routes_ref[i, r], jnp.int32).astype(f32)
            row = jnp.where(lane_row == s * req + r, value, row)
        route_rows.append(row)
    rest = qbuf.shape[1] - strips * req - 2
    qbuf[s] = jnp.concatenate(
        packed(q, strips) + route_rows + [jnp.zeros((rest, LANES), f32)], axis=0
    ).astype(bf16)

    stream = stream_ref[...].astype(f32)
    part = stream[:, 0:width]
    gains = gain_ref[...].reshape(1, -1)
    gain = gains[:, 0:width]
    for i in range(1, n_tensor):
        here = t == i
        part = jnp.where(here, stream[:, i * width : (i + 1) * width], part)
        gain = jnp.where(here, gains[:, i * width : (i + 1) * width], gain)
    vn = vn_ref[...].astype(f32)
    rest = ebuf.shape[1] - 2 * strips * req
    ebuf[s] = jnp.concatenate(
        packed(part, strips) + packed(vn, strips) + [jnp.zeros((rest, LANES), f32)], axis=0
    ).astype(bf16)

    pl.semaphore_wait(barrier, total_devices - 1)
    gather_start(qbuf, qs, qr)
    gather_start(ebuf, es, er)

    wg[:, ff:] = jnp.zeros((wg.shape[0], wg.shape[1] - ff), bf16)
    wu[:, ff:] = jnp.zeros((wu.shape[0], wu.shape[1] - ff), bf16)
    wd[:, ff:] = jnp.zeros((wd.shape[0], wd.shape[1] - ff), bf16)

    head_of = iota((width, LANES), 0) - HEAD_DIM * (iota((width, LANES), 1) - 16)
    to_own = ((head_of >= 0) & (head_of < HEAD_DIM)).astype(f32)
    from_head = iota((LANES, width), 1) - HEAD_DIM * iota((LANES, width), 0)
    spread = ((from_head >= 0) & (from_head < HEAD_DIM)).astype(f32)
    product = jnp.concatenate(
        [q * kn_ref[...].astype(f32), jnp.zeros((8 - req, width), f32)], axis=0
    )
    own_row = dot(product, to_own, HIGH)[0:req] * (1.0 / math.sqrt(HEAD_DIM))

    ph = pages * hp
    sub = iota((ph, 1), 0)
    page_row = sub >> 4
    head_row = sub & 15
    target = jnp.zeros((ph, 1), jnp.int32)
    high = jnp.zeros((ph, 1), jnp.int32)
    for p in range(pages):
        owner = owner_ref[s * pages + p]
        home = lax.div(owner, req)
        target = jnp.where(
            page_row == p, home * qbuf.shape[1] + (owner - home * req), target
        )
        high = jnp.where(page_row == p, p * slots + fill_ref[p], high)
    lane = iota((ph, pages * slots), 1)
    valid = (lane >= page_row * slots) & (lane < high)
    channel = iota((ph, width), 1) - HEAD_DIM * head_row
    head_mask = ((channel >= 0) & (channel < HEAD_DIM)).astype(f32)
    qlane = iota((ph, n_seq * qbuf.shape[1]), 1)
    picks = [(qlane == target + req * j).astype(bf16) for j in range(strips)]

    all_pages = pages * n_seq
    sub_r = iota((requests, LANES), 0)
    lane_r = iota((requests, LANES), 1)
    hot_pr = jnp.zeros((requests, LANES), f32)
    hot_rp = jnp.zeros((requests, LANES), f32)
    for p in range(all_pages):
        owner = owner_ref[p]
        hot_pr = jnp.where((sub_r == p) & (lane_r == owner), 1.0, hot_pr)
        hot_rp = jnp.where((sub_r == owner) & (lane_r == p), 1.0, hot_rp)
    hot_pr = hot_pr[:, 0:requests]
    hot_rp = hot_rp[:, 0:all_pages]

    loads[0].wait()
    gather_wait(qbuf, qs, qr)
    queries = qbuf[...].reshape(n_seq * qbuf.shape[1], LANES)
    page_q = jnp.concatenate([dot(pick, queries) for pick in picks], axis=1)[:, 0:width]
    page_q = (page_q * head_mask).astype(bf16)
    keys = kc[...].reshape(pages * slots, width)
    scores = lax.dot_general(
        page_q, keys, (((1,), (1,)), ((), ())), preferred_element_type=f32
    ) * (1.0 / math.sqrt(HEAD_DIM))
    scores = jnp.where(valid, scores, low_value)
    page_top = jnp.max(scores, axis=1, keepdims=True)
    weights = jnp.exp(scores - page_top)
    page_sum = jnp.sum(weights, axis=1, keepdims=True)
    loads[1].wait()
    values = vc[...].reshape(pages * slots, width)
    page_acc = dot(weights.astype(bf16), values) * (head_mask * (1.0 / page_sum))
    page_acc = jnp.sum(page_acc.reshape(pages, hp, width), axis=1)
    level = page_top + jnp.log(page_sum)
    level = jnp.where(iota((ph, LANES), 1) == head_row, level, 0.0)
    level = jnp.sum(level.reshape(pages, hp, LANES), axis=1)
    bbuf[s] = jnp.concatenate(packed(page_acc, strips) + [level + own_row], axis=0)
    gather_start(bbuf, bs, br)

    routed = qbuf[0, 16:32, :].astype(f32)
    for i in range(1, n_seq):
        routed = routed + qbuf[i, 16:32, :].astype(f32)
    first = strips * req - 16
    expert = jnp.full((1, LANES), s, jnp.int32).astype(f32)
    chosen = jnp.where(
        (routed[first : first + 1] == expert) | (routed[first + 1 : first + 2] == expert),
        1.0,
        0.0,
    )
    lane_1 = iota((1, LANES), 1)
    chosen = jnp.where(lane_1 < requests, chosen, 0.0)
    before_a = iota((LANES, LANES), 0)
    before_b = iota((LANES, LANES), 1)
    before = ((before_a < before_b) & ((before_a >> 2) == (before_b >> 2))).astype(bf16)
    rank = dot(jnp.broadcast_to(chosen, (16, LANES)).astype(bf16), before)
    slot_row = iota((rows, LANES), 0)
    slot_lane = iota((rows, LANES), 1)
    place = jnp.where(
        ((slot_lane >> 2) == (slot_row >> 1))
        & (rank == (slot_row & 1).astype(f32)),
        jnp.broadcast_to(chosen, (rows, LANES)),
        0.0,
    )[:, 0:requests].astype(bf16)

    home_row = iota((8, requests), 0)
    at_home = ((iota((8, requests), 1) == home_row + s * req) & (home_row < req)).astype(bf16)

    gather_wait(ebuf, es, er)

    def unpacked(buf, offset, kind):
        return jnp.concatenate(
            [
                jnp.concatenate(
                    [
                        buf[i].astype(f32)[offset + j * req : offset + (j + 1) * req]
                        for i in range(n_seq)
                    ],
                    axis=0,
                )
                for j in range(strips)
            ],
            axis=1,
        )[:, 0:width].astype(kind)

    stream_rows = dot(place, unpacked(ebuf, 0, bf16))
    new_values = unpacked(ebuf, strips * req, f32)

    gather_wait(bbuf, bs, br)
    levels = jnp.concatenate([bbuf[i, strips * req :, :] for i in range(n_seq)], axis=0)
    own = jnp.concatenate([levels[:, 16:], levels[:, 0:16]], axis=1)
    top = own
    for p in range(all_pages):
        top = jnp.maximum(top, jnp.where(sub_r == owner_ref[p], levels[p : p + 1], low_value))
    factor = jnp.exp(levels - dot(hot_pr, top, HIGH))
    own_factor = jnp.exp(own - top)
    wide = dot(jnp.concatenate([factor, own_factor], axis=0), spread, HIGH)
    page_wide, own_wide = wide[0:all_pages], wide[all_pages:]
    acc = dot(hot_rp, page_wide * unpacked(bbuf, 0, f32), HIGH) + own_wide * new_values
    total = 1.0 / (dot(hot_rp, factor, HIGH) + own_factor)
    attended = (acc * dot(total, spread, HIGH)).astype(bf16)

    loads[2].wait()
    projected = dot_t(attended, ow[...])
    psend[...] = jnp.concatenate(
        [projected, jnp.zeros((requests, psend.shape[1] - cols), f32)], axis=1
    ).astype(bf16)
    ratio = n_seq // n_tensor
    column = s // ratio
    pslot = lax.rem(s, ratio) * n_tensor + t

    def part_copy(k):
        return pltpu.make_async_remote_copy(
            src_ref=psend,
            dst_ref=precv.at[pslot],
            send_sem=ps.at[k],
            recv_sem=pr.at[pslot],
            device_id=(lax.rem(s + k, n_seq), column),
            device_id_type=MESH,
        )

    def self_part():
        return pltpu.make_async_copy(psend, precv.at[pslot], pr.at[pslot])

    for k in range(1, n_seq):
        part_copy(k).start()

    @pl.when(column != t)
    def _():
        part_copy(0).start()

    @pl.when(column == t)
    def _():
        self_part().start()

    halves = []
    for half in range(ratio):
        piece = None
        for i in range(n_tensor):
            j = half * n_tensor + i
            pltpu.make_async_copy(psend, precv.at[j], pr.at[j]).wait()
            term = precv[j].astype(f32)
            piece = term if piece is None else piece + term
        halves.append(piece[:, 0:cols])
    attn = jnp.concatenate(halves, axis=1).astype(bf16)

    resid = stream_rows + dot(place, attn)
    ssq[0] = jnp.broadcast_to(jnp.sum(resid * resid, axis=1, keepdims=True), (rows, LANES))
    x = (resid * gain).astype(bf16)

    low = lax.rem(t, 2)
    partners = [t, t + 1 - 2 * low, lax.rem(t + 2, 4), 3 - t]

    def tensor_copy(src, dst, send, recv, k, slot):
        return pltpu.make_async_remote_copy(
            src_ref=src,
            dst_ref=dst,
            send_sem=send.at[k],
            recv_sem=recv.at[slot],
            device_id=(s, partners[k]),
            device_id_type=MESH,
        )

    ssq_copies = [None] + [
        tensor_copy(ssq.at[0], ssq.at[k], ss, sr, k, k) for k in range(1, n_tensor)
    ]
    gate_copies = [None] + [
        tensor_copy(gsend.at[k], grecv.at[k], gs, gr, k, k) for k in range(1, n_tensor)
    ]
    for k in range(1, n_tensor):
        ssq_copies[k].start()
    loads[3].wait()
    loads[4].wait()
    for k in (2, 3, 1, 0):
        span = pl.ds(pl.multiple_of(partners[k] * chunk, LANES), chunk)
        gate = dot(x, wg[:, span])
        up = dot(x, wu[:, span])
        if k:
            gsend[k, 0] = gate.astype(bf16)
            gsend[k, 1] = up.astype(bf16)
            gate_copies[k].start()

    out_ref[0] = dot(at_home, attn)[0:req].astype(bf16)
    mean = ssq[0]
    for k in (1, 2, 3):
        ssq_copies[k].wait_recv()
        mean = mean + ssq[k]
    root = lax.rsqrt(mean[:, 0:1] * (1.0 / (width * n_tensor)) + eps)
    for k in (1, 2, 3):
        gate_copies[k].wait_recv()
        gate = gate + grecv[k, 0].astype(f32)
        up = up + grecv[k, 1].astype(f32)
    gate = gate * root
    up = up * root
    hid[0] = (gate / (1.0 + jnp.exp(-gate)) * up).astype(bf16)
    hid_copies = [None] + [
        tensor_copy(hid.at[0], hid.at[k], hs, hr, k, k) for k in range(1, n_tensor)
    ]
    for k in (2, 3, 1):
        hid_copies[k].start()

    wsub = iota((8 * strips, LANES), 0)
    wlane = iota((8 * strips, LANES), 1) - CAP * (wsub >> 3)
    mix = jnp.zeros((8 * strips, LANES), f32)
    for r in range(req):
        for i in range(2):
            e = routes_ref[i, r]
            taken = jnp.int32(0)
            for r2 in range(r):
                for i2 in range(2):
                    taken = taken + (routes_ref[i2, r2] == e).astype(jnp.int32)
            mix = jnp.where(
                ((wsub & 7) == r) & (wlane == e * 16 + taken), rw_ref[i, r], mix
            )

    loads[5].wait()
    out = None
    for k in (0, 1, 2, 3):
        if k:
            hid_copies[k].wait_recv()
        span = pl.ds(pl.multiple_of(partners[k] * chunk, LANES), chunk)
        term = dot_t(hid[k], wd[:, span])
        out = term if out is None else out + term

    tiles = packed(out, strips)
    fill = jnp.zeros((16 - CAP * strips, LANES), f32)
    for d in range(n_seq):
        osend[d] = jnp.concatenate(
            [tile[CAP * d : CAP * (d + 1)] for tile in tiles] + [fill], axis=0
        ).astype(bf16)
    for k in range(1, n_seq):
        peer = lax.rem(s + k, n_seq)
        seq_copy(osend.at[peer], orecv.at[s], os_, or_, k, s).start()
    orecv[s] = osend[s]
    for k in range(1, n_seq):
        peer = lax.rem(s + k, n_seq)
        seq_copy(osend.at[peer], orecv.at[peer], os_, or_, k, peer).wait_recv()
    returned = orecv[...].astype(f32).reshape(n_seq * 16, LANES)
    mixed = dot(mix, returned, HIGH)
    moe = jnp.concatenate([mixed[8 * j : 8 * j + req] for j in range(strips)], axis=1)
    out_ref[1] = moe[:, 0:width].astype(bf16)

    gather_sent(qbuf, qs, qr)
    gather_sent(ebuf, es, er)
    gather_sent(bbuf, bs, br)
    for k in range(1, n_seq):
        part_copy(k).wait_send()

    @pl.when(column != t)
    def _():
        part_copy(0).wait_send()

    for k in range(1, n_tensor):
        ssq_copies[k].wait_send()
        gate_copies[k].wait_send()
        hid_copies[k].wait_send()
    for k in range(1, n_seq):
        peer = lax.rem(s + k, n_seq)
        seq_copy(osend.at[peer], orecv.at[s], os_, or_, k, s).wait_send()


def one_kernel(n_seq, n_tensor, *args):
    (
        stream,
        new_query,
        k_new,
        v_new,
        k_cache,
        v_cache,
        page_owner,
        page_fill,
        out_weight,
        norm_gain,
        routes,
        route_weight,
        w_gate,
        w_up,
        w_down,
    ) = args
    req, width = new_query.shape
    ff = w_gate.shape[2]
    cols = out_weight.shape[1]
    requests = req * n_seq
    strips = -(-width // LANES)
    chunk = -(-ff // (n_tensor * LANES)) * LANES
    rows = n_seq * CAP
    smem = pl.BlockSpec(memory_space=pltpu.SMEM)
    vmem = pl.BlockSpec(memory_space=pltpu.VMEM)
    hbm = pl.BlockSpec(memory_space=pl.ANY)
    dma = pltpu.SemaphoreType.DMA
    out = jax.ShapeDtypeStruct((2, req, width), bf16)
    both = pl.pallas_call(
        functools.partial(layer_kernel, n_seq, n_tensor),
        out_shape=out,
        in_specs=[smem] * 4 + [vmem] * 5 + [hbm] * 6,
        out_specs=vmem,
        scratch_shapes=[
            pltpu.VMEM(k_cache.shape, bf16),
            pltpu.VMEM(v_cache.shape, bf16),
            pltpu.VMEM((cols, width), bf16),
            pltpu.VMEM((width, chunk * n_tensor), bf16),
            pltpu.VMEM((width, chunk * n_tensor), bf16),
            pltpu.VMEM((width, chunk * n_tensor), bf16),
            pltpu.VMEM((n_seq, 32, LANES), bf16),
            pltpu.VMEM((n_seq, 48, LANES), bf16),
            pltpu.VMEM((n_seq, 24, LANES), f32),
            pltpu.VMEM((requests, -(-cols // LANES) * LANES), bf16),
            pltpu.VMEM((n_seq, requests, -(-cols // LANES) * LANES), bf16),
            pltpu.VMEM((n_tensor, rows, LANES), f32),
            pltpu.VMEM((n_tensor, 2, rows, chunk), bf16),
            pltpu.VMEM((n_tensor, 2, rows, chunk), bf16),
            pltpu.VMEM((n_tensor, rows, chunk), bf16),
            pltpu.VMEM((n_seq, 16, LANES), bf16),
            pltpu.VMEM((n_seq, 16, LANES), bf16),
            dma((6,)),
        ]
        + [dma((n_seq,))] * 8
        + [dma((n_tensor,))] * 6
        + [dma((n_seq,))] * 2,
        compiler_params=pltpu.CompilerParams(
            collective_id=0, has_side_effects=True, vmem_limit_bytes=56 * 1024 * 1024
        ),
        name="layer",
    )(
        page_owner,
        page_fill,
        routes.T,
        route_weight.T,
        new_query,
        k_new,
        v_new,
        stream,
        norm_gain,
        k_cache,
        v_cache,
        out_weight.T,
        w_gate,
        w_up,
        jnp.swapaxes(w_down, 1, 2),
    )
    return both[0], both[1]


def fits_one_kernel(n_seq, n_tensor, args):
    req, width = args[1].shape
    pages = args[4].shape[0]
    strips = -(-width // LANES)
    return (
        n_seq == EXPERTS
        and n_tensor == 4
        and req == 4
        and pages == 4
        and strips == 5
        and width % HEAD_DIM == 0
        and width // HEAD_DIM <= 16
        and args[8].shape[1] * (n_seq // n_tensor) == width
    )


def either(n_seq, n_tensor, *args):
    if fits_one_kernel(n_seq, n_tensor, args):
        return one_kernel(n_seq, n_tensor, *args)
    return per_device(*args)


def solution(mesh):
    in_specs = (
        P("seq", None),
        P("seq", "tensor"),
        P("seq", "tensor"),
        P("seq", "tensor"),
        P("seq", None, "tensor"),
        P("seq", None, "tensor"),
        P(),
        P("seq"),
        P("tensor", "seq"),
        P(),
        P("seq", None),
        P("seq", None),
        P("seq", "tensor", None),
        P("seq", "tensor", None),
        P("seq", None, "tensor"),
    )
    out_specs = (P("seq", "tensor"), P("seq", "tensor"))
    return jax.shard_map(
        functools.partial(either, mesh.shape["seq"], mesh.shape["tensor"]), mesh=mesh, in_specs=in_specs, out_specs=out_specs, check_vma=False
    )
```
